32 devices in a mesh: group: 2 (over x), row: 16 (over z, y, core).
Axes of the slice: x: 2, y: 2, z: 4, core: 2. Of those that a mesh axis runs over, the one named last changes fastest.
Arguments:
- pair_act: bfloat16 [1024, 512, 128], P(('group', 'row')), parts along dimension 0, may hold values from -6 to 6
- res_mask: int32 [1024], P('group'), parts along dimension 0, may hold values 0 or 1
- w_left: bfloat16 [128, 256], replicated, may hold values from -0.5 to 0.5
- w_right: bfloat16 [128, 256], replicated, may hold values from -0.5 to 0.5
- w_gate: bfloat16 [128, 128], replicated, may hold values from -0.5 to 0.5
- w_out: bfloat16 [128, 128], replicated, may hold values from -0.5 to 0.5
Outputs:
- update: bfloat16 [1024, 512, 128], P(('group', 'row')), parts along dimension 0
The draws below stay inside these ranges and needn't reach their ends.
There are 2 independent parts, one for each index of `group`. The reference program is written for one: setup_inputs(seed, part) draws one part's arguments, and reference() takes and returns one part's arrays. A program takes and returns all parts, laid end to end along the dimension named above; an argument that names none is the same for every part. Nothing has to cross between parts.
All inputs are finite; a program needn't handle non-finite values.
Results may differ from the reference program's by a relative error of at most 0.0082.
Values may be sent and summed in bfloat16 or wider, within the bound.
A program may use at most 192 MiB of HBM per device.

```python
import jax
import jax.numpy as jnp
from jax import lax

C_Z = 128
C_HID = 128
RES_DEV = 32
N_RES = 512
N_ROW = 16


def plant(array, key, low, top_value):
    extent = array.shape
    place = [jax.random.randint(jax.random.fold_in(key, axis), (), 0, extent[axis]) for axis in range(len(extent))]
    array = array.at[tuple(place)].set(low)
    longest = extent.index(max(extent))
    place[longest] = (place[longest] + 1) % extent[longest]
    return array.at[tuple(place)].set(top_value)


def block_levels(key, extent, pieces, low, largest):
    factor_of, own = 1.0, jax.random.fold_in(key, 6)
    for axis_at, parts in pieces:
        heights = jnp.exp(jax.random.uniform(jax.random.fold_in(own, axis_at), (parts,), jnp.float32, low / len(pieces), largest / len(pieces)))
        factor_of = factor_of * jnp.repeat(heights, extent[axis_at] // parts).reshape([-1 if axis == axis_at else 1 for axis in range(len(extent))])
    return factor_of


def scatter_about(stream_key, dims, spread, bound, shards=(), held_as=jnp.bfloat16):
    values = jax.random.normal(stream_key, dims, jnp.float32) * spread
    if len(shards) > 0:
        values = block_levels(stream_key, dims, shards, -0.22, 0.18) * values
    return jnp.clip(values, min=-bound, max=bound).astype(held_as)


def setup_inputs(seed: int = 0, part: int = 0) -> dict:
    keys = jax.random.split(jax.random.key(seed), 7)
    own_keys = jax.random.split(jax.random.fold_in(keys[6], part), 7)
    pair_act = scatter_about(own_keys[0], (N_RES, N_RES, C_Z), 1.0, 6.0, ((0, 16),))
    res_mask = plant((jax.random.randint(own_keys[1], (N_RES,), 0, 8) < 7).astype(jnp.int32), jax.random.fold_in(own_keys[1], 1), 0, 1)
    w_left = scatter_about(keys[2], (C_Z, 2 * C_HID), C_Z ** -0.5, 0.5)
    w_right = scatter_about(keys[3], (C_Z, 2 * C_HID), C_Z ** -0.5, 0.5)
    w_gate = scatter_about(keys[4], (C_Z, C_Z), C_Z ** -0.5, 0.5)
    w_out = scatter_about(keys[5], (C_HID, C_Z), C_HID ** -0.5, 0.5)
    return {"pair_act": pair_act, "res_mask": res_mask, "w_left": w_left, "w_right": w_right, "w_gate": w_gate, "w_out": w_out}


EPS = 1e-05

def layer_norm(values, axis):
    average = lax.optimization_barrier(jnp.mean(values, axis=axis, keepdims=True))
    centred = values - average
    variance = lax.optimization_barrier(jnp.mean(centred * centred, axis=axis, keepdims=True))
    return centred * lax.rsqrt(variance + EPS)

def gated_side(normed_rows, weight, mask_rows, full_mask):
    hidden = jnp.einsum('rnd,de->ern', normed_rows.astype(jnp.float32), weight.astype(jnp.float32), precision=lax.Precision.HIGHEST)
    width = weight.shape[1] // 2
    gates = jax.nn.sigmoid(hidden[:width])
    masks = mask_rows.astype(jnp.float32)[None, :, None] * full_mask.astype(jnp.float32)[None, None, :]
    return (gates * hidden[width:] * masks).astype(jnp.bfloat16)

def reference(pair_act, res_mask, w_left, w_right, w_gate, w_out):
    blocks = pair_act.reshape(N_ROW, RES_DEV, N_RES, C_Z)
    mask_blocks = res_mask.reshape(N_ROW, RES_DEV)

    def sides(item):
        rows, mask_rows = item
        normed = layer_norm(rows.astype(jnp.float32), 2).astype(jnp.bfloat16)
        return (gated_side(normed, w_left, mask_rows, res_mask), gated_side(normed, w_right, mask_rows, res_mask))
    left_blocks, right_blocks = lax.map(sides, (blocks, mask_blocks))
    left_all = jnp.transpose(left_blocks, (1, 0, 2, 3)).reshape(C_HID, N_RES, N_RES)
    right_all = jnp.transpose(right_blocks, (1, 0, 2, 3)).reshape(C_HID, N_RES, N_RES)

    def contract(item):
        return jnp.dot(item[0], item[1].T, preferred_element_type=jnp.float32).astype(jnp.bfloat16)
    tri = lax.map(contract, (left_all, right_all))
    tri_blocks = jnp.transpose(tri.reshape(C_HID, N_ROW, RES_DEV, N_RES), (1, 0, 2, 3))

    def finish(item):
        rows, tri_rows = item
        normed = layer_norm(rows.astype(jnp.float32), 2).astype(jnp.bfloat16)
        gates = jax.nn.sigmoid(jnp.einsum('rnd,de->rne', normed.astype(jnp.float32), w_gate.astype(jnp.float32), precision=lax.Precision.HIGHEST))
        tri_normed = layer_norm(tri_rows.astype(jnp.float32), 0).astype(jnp.bfloat16)
        projected = jnp.einsum('crn,cd->rnd', tri_normed.astype(jnp.float32), w_out.astype(jnp.float32), precision=lax.Precision.HIGHEST)
        return (gates * projected).astype(jnp.bfloat16)
    update = lax.map(finish, (blocks, tri_blocks))
    return update.reshape(N_RES, N_RES, C_Z)
```

```python
import functools

import jax
import jax.numpy as jnp
from jax import lax
from jax.experimental import pallas as pl
from jax.experimental.pallas import tpu as pltpu
from jax.sharding import PartitionSpec as P

EPS = 1e-05
TILE = 16
LANES = 128
HALVES = 2
PITCH = 136
FPITCH = 24


def layer_norm(values, axis):
    average = jnp.mean(values, axis=axis, keepdims=True)
    centred = values - average
    variance = jnp.mean(centred * centred, axis=axis, keepdims=True)
    return centred * lax.rsqrt(variance + EPS)


def sigmoid(x):
    return 0.5 + 0.5 * jnp.tanh(0.5 * x)


def plain_body(pair_act, res_mask, w_left, w_right, w_gate, w_out):
    rows = pair_act.shape[0]
    width = w_left.shape[1] // 2
    first = lax.axis_index("row") * rows
    mask_rows = lax.dynamic_slice_in_dim(res_mask, first, rows)
    masks = (
        mask_rows.astype(jnp.float32)[None, :, None] * res_mask.astype(jnp.float32)[None, None, :]
    )
    normed = layer_norm(pair_act.astype(jnp.float32), 2).astype(jnp.bfloat16)

    def gated_side(weight):
        hidden = jnp.einsum("rnd,de->ern", normed, weight, preferred_element_type=jnp.float32)
        return (jax.nn.sigmoid(hidden[:width]) * hidden[width:] * masks).astype(jnp.bfloat16)

    left_edges = gated_side(w_left)
    right_edges = gated_side(w_right)
    left_cols, right_cols = (
        lax.all_to_all(left_edges, "row", split_axis=0, concat_axis=1, tiled=True),
        lax.all_to_all(right_edges, "row", split_axis=0, concat_axis=1, tiled=True),
    )
    tri_cols = jnp.einsum(
        "cik,cjk->cij", left_cols, right_cols, preferred_element_type=jnp.float32
    ).astype(jnp.bfloat16)
    tri_rows = lax.all_to_all(tri_cols, "row", split_axis=1, concat_axis=0, tiled=True)
    gates = jax.nn.sigmoid(
        jnp.einsum("rnd,de->rne", normed, w_gate, preferred_element_type=jnp.float32)
    )
    tri_normed = layer_norm(tri_rows.astype(jnp.float32), 0).astype(jnp.bfloat16)
    projected = jnp.einsum("crn,cd->rnd", tri_normed, w_out, preferred_element_type=jnp.float32)
    return (gates * projected).astype(jnp.bfloat16)


def kernel(
    n, pair, mask_s, mask_v, wt, w_gate, w_out, out,
    normed, own_l, own_r, got_l, got_r, tri, got_t, stage, turn,
    sem_l, sem_r, sem_t, out_l, out_r, out_t,
):
    rows, _, blocks, _, _ = pair.shape
    width = own_l.shape[0]
    length = own_l.shape[2]
    peers = n // HALVES
    share = width // peers
    lane_tiles = length // LANES
    block_devs = LANES // (TILE * blocks)
    me = lax.axis_index("row")
    half = me // peers
    spot = lax.rem(me, peers)

    barrier = pltpu.get_barrier_semaphore()
    for step in range(1, n):
        pl.semaphore_signal(barrier, inc=1, device_id={"row": lax.rem(me + step, n)})
    pl.semaphore_wait(barrier, n - 1)

    def remote(src, dst, send, recv, device):
        pltpu.make_async_remote_copy(
            src_ref=src, dst_ref=dst, send_sem=send, recv_sem=recv, device_id={"row": device}
        ).start()

    def edges(block):
        def one_row(r, carry):
            row = block * TILE + r
            mask_i = mask_s[me * rows + row].astype(jnp.float32)
            for kt in range(lane_tiles):
                devs = pl.ds(kt * block_devs, block_devs)
                x = pair[row, devs].reshape(LANES, -1).astype(jnp.float32)
                nrm = layer_norm(x, 1).astype(jnp.bfloat16)
                normed[row, devs] = nrm.reshape(block_devs, blocks, TILE, -1)
                h = lax.dot_general(
                    wt[...], nrm, (((1,), (1,)), ((), ())), preferred_element_type=jnp.float32
                )
                mask_k = mask_v[:, kt * LANES : (kt + 1) * LANES].astype(jnp.float32) * mask_i
                for side in range(2):
                    gate = h[side * 2 * width : (side * 2 + 1) * width]
                    value = h[(side * 2 + 1) * width : (side * 2 + 2) * width]
                    stage[kt, side, pl.ds(r * PITCH, width), :] = sigmoid(gate) * value * mask_k
            return carry

        lax.fori_loop(0, TILE, one_row, 0)

        def one_channel(c, carry):
            for side, own in enumerate((own_l, own_r)):
                for kt in range(lane_tiles):
                    v = stage[kt, side, pl.ds(c, TILE, stride=PITCH), :]
                    own[c, block * TILE : (block + 1) * TILE, kt * LANES : (kt + 1) * LANES] = (
                        v.astype(jnp.bfloat16)
                    )
            return carry

        lax.fori_loop(0, width, one_channel, 0, unroll=4)

    def piece(ref, at, block):
        return ref.at[pl.ds(at * share, share), pl.ds(block * TILE, TILE)]

    def send_edges(block):
        for step in range(peers):
            to = lax.rem(spot + step, peers)
            remote(
                piece(own_r, to, block), got_r.at[block, 1, :, pl.ds(spot * TILE, TILE)],
                out_r.at[block], sem_r.at[block, 1], (1 - half) * peers + to,
            )
        l_dst = got_l.at[:, pl.ds(spot * rows + block * TILE, TILE)]
        r_dst = got_r.at[block, 0, :, pl.ds(spot * TILE, TILE)]
        for step in range(1, peers):
            to = lax.rem(spot + step, peers)
            remote(piece(own_l, to, block), l_dst, out_l, sem_l, half * peers + to)
            remote(
                piece(own_r, to, block), r_dst, out_r.at[block], sem_r.at[block, 0],
                half * peers + to,
            )
        pltpu.make_async_copy(piece(own_l, spot, block), l_dst, sem_l).start()
        pltpu.make_async_copy(piece(own_r, spot, block), r_dst, sem_r.at[block, 0]).start()

    def contract(block, rel):
        pltpu.make_async_copy(
            got_r.at[block, rel], got_r.at[block, rel], sem_r.at[block, rel]
        ).wait()

        def one(c, carry):
            tri[block, rel, c] = lax.dot_general(
                got_l[c], got_r[block, rel, c], (((1,), (1,)), ((), ())),
                preferred_element_type=jnp.float32,
            ).astype(jnp.bfloat16)
            return carry

        lax.fori_loop(0, share, one, 0)
        dst = got_t.at[block, rel, pl.ds(spot * share, share)]
        for step in range(1, peers):
            to = lax.rem(spot + step, peers)
            remote(
                tri.at[block, rel, :, pl.ds(to * rows, rows)], dst,
                out_t.at[block, rel], sem_t.at[block, rel], half * peers + to,
            )
        pltpu.make_async_copy(
            tri.at[block, rel, :, pl.ds(spot * rows, rows)], dst, sem_t.at[block, rel]
        ).start()

    def finish(block, rel):
        pltpu.make_async_copy(
            got_t.at[block, rel], got_t.at[block, rel], sem_t.at[block, rel]
        ).wait()
        source = lax.rem(half + rel, HALVES)
        devs = pl.ds(source * peers, peers)
        for ib in range(rows // TILE):
            i_rows = pl.ds(ib * TILE, TILE)

            def load(c):
                return got_t[block, rel, c, i_rows, :].astype(jnp.float32)

            zero = jnp.zeros((TILE, peers * TILE), jnp.float32)
            mean = lax.fori_loop(0, width, lambda c, s: s + load(c), zero, unroll=8) * (1.0 / width)

            def spread(c, s):
                d = load(c) - mean
                return s + d * d

            var = lax.fori_loop(0, width, spread, zero, unroll=8) * (1.0 / width)
            scale = lax.rsqrt(var + EPS)

            def put(c, carry):
                turn[pl.ds(c * FPITCH, TILE), :] = (load(c) - mean) * scale
                return carry

            lax.fori_loop(0, width, put, 0, unroll=8)

            def one_row(i, carry):
                row = ib * TILE + i
                tn = turn[pl.ds(i, width, stride=FPITCH), :].astype(jnp.bfloat16)
                projected = lax.dot_general(
                    tn, w_out[...], (((0,), (0,)), ((), ())), preferred_element_type=jnp.float32
                )
                nrm = normed[row, devs, block].reshape(peers * TILE, -1)
                gates = sigmoid(jnp.dot(nrm, w_gate[...], preferred_element_type=jnp.float32))
                out[row, devs, block] = (
                    (gates * projected).astype(jnp.bfloat16).reshape(peers, TILE, -1)
                )
                return carry

            lax.fori_loop(0, TILE, one_row, 0, unroll=2)

    for block in range(blocks):
        edges(block)
        send_edges(block)
    pltpu.make_async_copy(got_l, got_l, sem_l).wait()
    steps = [(block, rel) for rel in range(HALVES) for block in range(blocks)]
    for at, step in enumerate(steps):
        contract(*step)
        if at >= 1:
            finish(*steps[at - 1])
    finish(*steps[-1])

    rest = (peers - 1) * share
    l_sent = own_l.at[pl.ds(0, rest)]
    pltpu.make_async_copy(l_sent, l_sent, out_l).wait()
    for block in range(blocks):
        both = own_r.at[pl.ds(0, width - share // 2)]
        pltpu.make_async_copy(both, both, out_r.at[block]).wait()
        for rel in range(HALVES):
            t_sent = tri.at[block, rel, :, pl.ds(0, (peers - 1) * rows)]
            pltpu.make_async_copy(t_sent, t_sent, out_t.at[block, rel]).wait()


def fused_body(n, pair_act, res_mask, w_left, w_right, w_gate, w_out):
    rows, length, depth = pair_act.shape
    width = w_left.shape[1] // 2
    peers = n // HALVES
    share = width // peers
    blocks = rows // TILE
    bf16 = jnp.bfloat16
    wt = jnp.concatenate([w_left, w_right], axis=1).T
    view = (rows, n, blocks, TILE, depth)
    vmem = pl.BlockSpec(memory_space=pltpu.VMEM)
    dma = pltpu.SemaphoreType.DMA
    result = pl.pallas_call(
        functools.partial(kernel, n),
        out_shape=jax.ShapeDtypeStruct(view, bf16),
        in_specs=[vmem, pl.BlockSpec(memory_space=pltpu.SMEM)] + [vmem] * 4,
        out_specs=vmem,
        scratch_shapes=[
            pltpu.VMEM(view, bf16),
            pltpu.VMEM((width, rows, length), bf16),
            pltpu.VMEM((width, rows, length), bf16),
            pltpu.VMEM((share, peers * rows, length), bf16),
            pltpu.VMEM((blocks, HALVES, share, peers * TILE, length), bf16),
            pltpu.VMEM((blocks, HALVES, share, peers * rows, peers * TILE), bf16),
            pltpu.VMEM((blocks, HALVES, width, rows, peers * TILE), bf16),
            pltpu.VMEM((length // LANES, 2, TILE * PITCH, LANES), jnp.float32),
            pltpu.VMEM((width * FPITCH, LANES), jnp.float32),
            dma,
            dma((blocks, HALVES)),
            dma((blocks, HALVES)),
            dma,
            dma((blocks,)),
            dma((blocks, HALVES)),
        ],
        compiler_params=pltpu.CompilerParams(
            collective_id=0, has_side_effects=True, vmem_limit_bytes=62 * 2**20
        ),
    )(pair_act.reshape(view), res_mask, res_mask.reshape(1, length), wt, w_gate, w_out)
    return result.reshape(rows, length, depth)


def body(n, pair_act, *others):
    rows, length, depth = pair_act.shape
    fits = rows == 2 * TILE and n // HALVES * TILE == LANES and depth == LANES and length == n * rows
    if fits and others[1].shape[1] == 2 * LANES:
        return fused_body(n, pair_act, *others)
    return plain_body(pair_act, *others)


def solution(mesh):
    placed = (P(("group", "row"), None, None), P("group"), P(), P(), P(), P())
    return jax.shard_map(
        functools.partial(body, mesh.shape["row"]), mesh=mesh, in_specs=placed,
        out_specs=P(("group", "row"), None, None), check_vma=False,
    )
```

```python
import functools

import jax
import jax.numpy as jnp
from jax import lax
from jax.experimental import pallas as pl
from jax.experimental.pallas import tpu as pltpu
from jax.sharding import PartitionSpec as P

EPS = 1e-05
TILE = 16
LANES = 128
HALVES = 2
PITCH = 136
FPITCH = 24


def layer_norm(values, axis):
    average = jnp.mean(values, axis=axis, keepdims=True)
    centred = values - average
    variance = jnp.mean(centred * centred, axis=axis, keepdims=True)
    return centred * lax.rsqrt(variance + EPS)


def sigmoid(x):
    return 0.5 + 0.5 * jnp.tanh(0.5 * x)


def plain_body(pair_act, res_mask, w_left, w_right, w_gate, w_out):
    rows = pair_act.shape[0]
    width = w_left.shape[1] // 2
    first = lax.axis_index("row") * rows
    mask_rows = lax.dynamic_slice_in_dim(res_mask, first, rows)
    masks = (
        mask_rows.astype(jnp.float32)[None, :, None] * res_mask.astype(jnp.float32)[None, None, :]
    )
    normed = layer_norm(pair_act.astype(jnp.float32), 2).astype(jnp.bfloat16)

    def gated_side(weight):
        hidden = jnp.einsum("rnd,de->ern", normed, weight, preferred_element_type=jnp.float32)
        return (jax.nn.sigmoid(hidden[:width]) * hidden[width:] * masks).astype(jnp.bfloat16)

    left_edges = gated_side(w_left)
    right_edges = gated_side(w_right)
    left_cols, right_cols = (
        lax.all_to_all(left_edges, "row", split_axis=0, concat_axis=1, tiled=True),
        lax.all_to_all(right_edges, "row", split_axis=0, concat_axis=1, tiled=True),
    )
    tri_cols = jnp.einsum(
        "cik,cjk->cij", left_cols, right_cols, preferred_element_type=jnp.float32
    ).astype(jnp.bfloat16)
    tri_rows = lax.all_to_all(tri_cols, "row", split_axis=1, concat_axis=0, tiled=True)
    gates = jax.nn.sigmoid(
        jnp.einsum("rnd,de->rne", normed, w_gate, preferred_element_type=jnp.float32)
    )
    tri_normed = layer_norm(tri_rows.astype(jnp.float32), 0).astype(jnp.bfloat16)
    projected = jnp.einsum("crn,cd->rnd", tri_normed, w_out, preferred_element_type=jnp.float32)
    return (gates * projected).astype(jnp.bfloat16)


def shares_of(width, peers):
    outer = width * 3 // (4 * peers)
    return outer, 2 * width // peers - outer


def kernel(
    n, pair, mask_s, mask_v, wt, w_gate, w_out, out,
    normed, own_l, own_r, got_l, got_r, tri, got_t, stage, turn,
    sem_l, sem_r, sem_t, out_l, out_r, out_x, out_t,
):
    rows, _, blocks, _, _ = pair.shape
    width = own_l.shape[0]
    length = own_l.shape[2]
    peers = n // HALVES
    plane = peers // 2
    shares = shares_of(width, peers)
    lane_tiles = length // LANES
    block_devs = LANES // (TILE * blocks)
    me = lax.axis_index("row")
    half = me // peers
    spot = lax.rem(me, peers)
    ring = lax.rem(spot + half * plane, peers)
    role = ring // plane
    lane = lax.rem(ring, plane)

    def device(which_half, cls, at):
        return which_half * peers + lax.rem(cls * plane + at + which_half * plane, peers)

    def first_channel(cls, at):
        return cls * plane * shares[0] + at * shares[cls]

    def by_role(act):
        for inner in range(2):
            pl.when(role == inner)(functools.partial(act, inner))

    barrier = pltpu.get_barrier_semaphore()
    for step in range(1, n):
        pl.semaphore_signal(barrier, inc=1, device_id={"row": lax.rem(me + step, n)})
    pl.semaphore_wait(barrier, n - 1)

    def remote(src, dst, send, recv, to):
        pltpu.make_async_remote_copy(
            src_ref=src, dst_ref=dst, send_sem=send, recv_sem=recv, device_id={"row": to}
        ).start()

    def wait(ref, sem):
        pltpu.make_async_copy(ref, ref, sem).wait()

    def edges(block):
        def one_row(r, carry):
            row = block * TILE + r
            mask_i = mask_s[me * rows + row].astype(jnp.float32)
            for kt in range(lane_tiles):
                devs = pl.ds(kt * block_devs, block_devs)
                x = pair[row, devs].reshape(LANES, -1).astype(jnp.float32)
                nrm = layer_norm(x, 1).astype(jnp.bfloat16)
                normed[row, devs] = nrm.reshape(block_devs, blocks, TILE, -1)
                h = lax.dot_general(
                    wt[...], nrm, (((1,), (1,)), ((), ())), preferred_element_type=jnp.float32
                )
                mask_k = mask_v[:, kt * LANES : (kt + 1) * LANES].astype(jnp.float32) * mask_i
                for side in range(2):
                    gate = h[side * 2 * width : (side * 2 + 1) * width]
                    value = h[(side * 2 + 1) * width : (side * 2 + 2) * width]
                    stage[kt, side, pl.ds(r * PITCH, width), :] = sigmoid(gate) * value * mask_k
            return carry

        lax.fori_loop(0, TILE, one_row, 0)

        def one_channel(c, carry):
            for side, own in enumerate((own_l, own_r)):
                for kt in range(lane_tiles):
                    v = stage[kt, side, pl.ds(c, TILE, stride=PITCH), :]
                    own[c, block * TILE : (block + 1) * TILE, kt * LANES : (kt + 1) * LANES] = (
                        v.astype(jnp.bfloat16)
                    )
            return carry

        lax.fori_loop(0, width, one_channel, 0, unroll=4)

    def send_edges(block, inner):
        sem_own = 0 if inner else 2
        row_block = pl.ds(block * TILE, TILE)
        l_rows = pl.ds(spot * rows + block * TILE, TILE)
        r_rows = pl.ds(spot * TILE, TILE)

        def targets(cls):
            for step in range(plane):
                at = lax.rem(lane + step, plane)
                local = cls == inner and step == 0
                yield at, local, pl.ds(first_channel(cls, at), shares[cls])

        def cross(cls):
            for at, _, channels in targets(cls):
                remote(
                    own_r.at[channels, row_block], got_r.at[block, 1, pl.ds(0, shares[cls]), r_rows],
                    out_r.at[block], sem_r.at[block, 1], device(1 - half, cls, at),
                )

        def own_right(cls):
            dst = got_r.at[block, 0, pl.ds(0, shares[cls]), r_rows]
            for at, local, channels in targets(cls):
                src = own_r.at[channels, row_block]
                if local:
                    pltpu.make_async_copy(src, dst, sem_r.at[block, sem_own]).start()
                else:
                    remote(
                        src, dst, out_r.at[block], sem_r.at[block, sem_own], device(half, cls, at)
                    )

        def own_left(cls):
            dst = got_l.at[pl.ds(0, shares[cls]), l_rows]
            for at, local, channels in targets(cls):
                src = own_l.at[channels, row_block]
                if local:
                    pltpu.make_async_copy(src, dst, sem_l).start()
                else:
                    remote(src, dst, out_l, sem_l, device(half, cls, at))

        if inner:
            cross(1)
            cross(0)
            own_right(0)
            own_right(1)
        else:
            own_right(1)
            cross(0)
            own_right(0)
        own_left(0)
        own_left(1)

    def forward(block, inner):
        if inner:
            part = got_r.at[
                block, 0, pl.ds(0, shares[1]), pl.ds(half * plane * TILE, plane * TILE)
            ]
            wait(part, sem_r.at[block, 2])
            remote(
                part,
                got_r.at[block, 1, pl.ds(0, shares[1]), pl.ds(half * plane * TILE, plane * TILE)],
                out_x.at[block], sem_r.at[block, 1], device(1 - half, 1, lane),
            )

    def contract(block, rel, inner):
        share = shares[inner]
        if rel:
            wait(got_r.at[block, 1, pl.ds(0, share)], sem_r.at[block, 1])
        else:
            part = got_r.at[block, 0, pl.ds(0, share), pl.ds(0, plane * TILE)]
            wait(part, sem_r.at[block, 0])
            if not inner:
                wait(part, sem_r.at[block, 2])

        def one(c, carry):
            tri[block, rel, c] = lax.dot_general(
                got_l[c], got_r[block, rel, c], (((1,), (1,)), ((), ())),
                preferred_element_type=jnp.float32,
            ).astype(jnp.bfloat16)
            return carry

        lax.fori_loop(0, share, one, 0)
        dst = got_t.at[block, rel, pl.ds(first_channel(inner, lane), share)]
        for step in range(1, peers):
            to = lax.rem(spot + step, peers)
            remote(
                tri.at[block, rel, pl.ds(0, share), pl.ds(to * rows, rows)], dst,
                out_t.at[block, rel], sem_t.at[block, rel], half * peers + to,
            )
        pltpu.make_async_copy(
            tri.at[block, rel, pl.ds(0, share), pl.ds(spot * rows, rows)], dst,
            sem_t.at[block, rel],
        ).start()

    def finish(block, rel):
        pltpu.make_async_copy(
            got_t.at[block, rel], got_t.at[block, rel], sem_t.at[block, rel]
        ).wait()
        source = lax.rem(half + rel, HALVES)
        devs = pl.ds(source * peers, peers)
        for ib in range(rows // TILE):
            i_rows = pl.ds(ib * TILE, TILE)

            def load(c):
                return got_t[block, rel, c, i_rows, :].astype(jnp.float32)

            zero = jnp.zeros((TILE, peers * TILE), jnp.float32)
            mean = lax.fori_loop(0, width, lambda c, s: s + load(c), zero, unroll=8) * (1.0 / width)

            def spread(c, s):
                d = load(c) - mean
                return s + d * d

            var = lax.fori_loop(0, width, spread, zero, unroll=8) * (1.0 / width)
            scale = lax.rsqrt(var + EPS)

            def put(c, carry):
                turn[pl.ds(c * FPITCH, TILE), :] = (load(c) - mean) * scale
                return carry

            lax.fori_loop(0, width, put, 0, unroll=8)

            def one_row(i, carry):
                row = ib * TILE + i
                tn = turn[pl.ds(i, width, stride=FPITCH), :].astype(jnp.bfloat16)
                projected = lax.dot_general(
                    tn, w_out[...], (((0,), (0,)), ((), ())), preferred_element_type=jnp.float32
                )
                nrm = normed[row, devs, block].reshape(peers * TILE, -1)
                gates = sigmoid(jnp.dot(nrm, w_gate[...], preferred_element_type=jnp.float32))
                out[row, devs, block] = (
                    (gates * projected).astype(jnp.bfloat16).reshape(peers, TILE, -1)
                )
                return carry

            lax.fori_loop(0, TILE, one_row, 0, unroll=2)

    for block in range(blocks):
        edges(block)
        by_role(functools.partial(send_edges, block))

    def ready(inner):
        for block in range(blocks):
            forward(block, inner)
        wait(got_l.at[pl.ds(0, shares[inner])], sem_l)

    by_role(ready)
    steps = [(block, rel) for rel in range(HALVES) for block in range(blocks)]
    for at, step in enumerate(steps):
        by_role(functools.partial(contract, *step))
        if at >= 1:
            finish(*steps[at - 1])
    finish(*steps[-1])

    def drain(inner):
        near = width - shares[inner]
        far = width if inner else plane * shares[0]
        wait(own_l.at[pl.ds(0, near)], out_l)
        for block in range(blocks):
            wait(own_r.at[pl.ds(0, (near + far) // 2)], out_r.at[block])
            if inner:
                wait(got_r.at[block, 0, pl.ds(0, shares[1]), pl.ds(0, plane * TILE)], out_x.at[block])
            for rel in range(HALVES):
                wait(
                    tri.at[block, rel, pl.ds(0, shares[inner]), pl.ds(0, (peers - 1) * rows)],
                    out_t.at[block, rel],
                )

    by_role(drain)


def fused_body(n, pair_act, res_mask, w_left, w_right, w_gate, w_out):
    rows, length, depth = pair_act.shape
    width = w_left.shape[1] // 2
    peers = n // HALVES
    share = max(shares_of(width, peers))
    blocks = rows // TILE
    bf16 = jnp.bfloat16
    wt = jnp.concatenate([w_left, w_right], axis=1).T
    view = (rows, n, blocks, TILE, depth)
    vmem = pl.BlockSpec(memory_space=pltpu.VMEM)
    dma = pltpu.SemaphoreType.DMA
    result = pl.pallas_call(
        functools.partial(kernel, n),
        out_shape=jax.ShapeDtypeStruct(view, bf16),
        in_specs=[vmem, pl.BlockSpec(memory_space=pltpu.SMEM)] + [vmem] * 4,
        out_specs=vmem,
        scratch_shapes=[
            pltpu.VMEM(view, bf16),
            pltpu.VMEM((width, rows, length), bf16),
            pltpu.VMEM((width, rows, length), bf16),
            pltpu.VMEM((share, peers * rows, length), bf16),
            pltpu.VMEM((blocks, HALVES, share, peers * TILE, length), bf16),
            pltpu.VMEM((blocks, HALVES, share, peers * rows, peers * TILE), bf16),
            pltpu.VMEM((blocks, HALVES, width, rows, peers * TILE), bf16),
            pltpu.VMEM((length // LANES, 2, TILE * PITCH, LANES), jnp.float32),
            pltpu.VMEM((width * FPITCH, LANES), jnp.float32),
            dma,
            dma((blocks, 3)),
            dma((blocks, HALVES)),
            dma,
            dma((blocks,)),
            dma((blocks,)),
            dma((blocks, HALVES)),
        ],
        compiler_params=pltpu.CompilerParams(
            collective_id=0, has_side_effects=True, vmem_limit_bytes=62 * 2**20
        ),
    )(pair_act.reshape(view), res_mask, res_mask.reshape(1, length), wt, w_gate, w_out)
    return result.reshape(rows, length, depth)


def body(n, pair_act, *others):
    rows, length, depth = pair_act.shape
    fits = rows == 2 * TILE and n // HALVES * TILE == LANES and depth == LANES and length == n * rows
    if fits and others[1].shape[1] == 2 * LANES:
        return fused_body(n, pair_act, *others)
    return plain_body(pair_act, *others)


def solution(mesh):
    placed = (P(("group", "row"), None, None), P("group"), P(), P(), P(), P())
    return jax.shard_map(
        functools.partial(body, mesh.shape["row"]), mesh=mesh, in_specs=placed,
        out_specs=P(("group", "row"), None, None), check_vma=False,
    )
```

```python
import functools

import jax
import jax.numpy as jnp
from jax import lax
from jax.experimental import pallas as pl
from jax.experimental.pallas import tpu as pltpu
from jax.sharding import PartitionSpec as P

EPS = 1e-05
TILE = 16
LANES = 128
HALVES = 2
PITCH = 136
FPITCH = 24
GROUPS = 4


def layer_norm(values, axis):
    average = jnp.mean(values, axis=axis, keepdims=True)
    centred = values - average
    variance = jnp.mean(centred * centred, axis=axis, keepdims=True)
    return centred * lax.rsqrt(variance + EPS)


def sigmoid(x):
    return 0.5 + 0.5 * jnp.tanh(0.5 * x)


def plain_body(pair_act, res_mask, w_left, w_right, w_gate, w_out):
    rows = pair_act.shape[0]
    width = w_left.shape[1] // 2
    first = lax.axis_index("row") * rows
    mask_rows = lax.dynamic_slice_in_dim(res_mask, first, rows)
    masks = (
        mask_rows.astype(jnp.float32)[None, :, None] * res_mask.astype(jnp.float32)[None, None, :]
    )
    normed = layer_norm(pair_act.astype(jnp.float32), 2).astype(jnp.bfloat16)

    def gated_side(weight):
        hidden = jnp.einsum("rnd,de->ern", normed, weight, preferred_element_type=jnp.float32)
        return (jax.nn.sigmoid(hidden[:width]) * hidden[width:] * masks).astype(jnp.bfloat16)

    left_edges = gated_side(w_left)
    right_edges = gated_side(w_right)
    left_cols, right_cols = (
        lax.all_to_all(left_edges, "row", split_axis=0, concat_axis=1, tiled=True),
        lax.all_to_all(right_edges, "row", split_axis=0, concat_axis=1, tiled=True),
    )
    tri_cols = jnp.einsum(
        "cik,cjk->cij", left_cols, right_cols, preferred_element_type=jnp.float32
    ).astype(jnp.bfloat16)
    tri_rows = lax.all_to_all(tri_cols, "row", split_axis=1, concat_axis=0, tiled=True)
    gates = jax.nn.sigmoid(
        jnp.einsum("rnd,de->rne", normed, w_gate, preferred_element_type=jnp.float32)
    )
    tri_normed = layer_norm(tri_rows.astype(jnp.float32), 0).astype(jnp.bfloat16)
    projected = jnp.einsum("crn,cd->rnd", tri_normed, w_out, preferred_element_type=jnp.float32)
    return (gates * projected).astype(jnp.bfloat16)


def shares_of(width, peers):
    outer = width * 3 // (4 * peers)
    return outer, 2 * width // peers - outer


def kernel(
    n, pair, mask_s, mask_v, w_left, w_right, w_gate, w_out, result,
    normed, own_l, own_r, got_l, got_r, tri, got_t, stage, turn, wt, out,
    sem_l, sem_r, sem_c, sem_t, out_l, out_r, out_x, out_t, sem_out,
):
    rows, _, blocks, _, _ = pair.shape
    width = own_l.shape[0]
    length = own_l.shape[2]
    peers = n // HALVES
    plane = peers // 2
    shares = shares_of(width, peers)
    lane_tiles = length // LANES
    block_devs = LANES // (TILE * blocks)
    me = lax.axis_index("row")
    half = me // peers
    spot = lax.rem(me, peers)
    ring = lax.rem(spot + half * plane, peers)
    role = ring // plane
    lane = lax.rem(ring, plane)

    def device(which_half, cls, at):
        return which_half * peers + lax.rem(cls * plane + at + which_half * plane, peers)

    def first_channel(cls, at):
        return cls * plane * shares[0] + at * shares[cls]

    def by_role(act):
        for inner in range(2):
            pl.when(role == inner)(functools.partial(act, inner))

    barrier = pltpu.get_barrier_semaphore()
    for step in range(1, n):
        pl.semaphore_signal(barrier, inc=1, device_id={"row": lax.rem(me + step, n)})
    for side, weight in enumerate((w_left, w_right)):
        wt[side] = weight[...].astype(jnp.float32).T.astype(jnp.bfloat16)

    def remote(src, dst, send, recv, to):
        pltpu.make_async_remote_copy(
            src_ref=src, dst_ref=dst, send_sem=send, recv_sem=recv, device_id={"row": to}
        ).start()

    def wait(ref, sem):
        pltpu.make_async_copy(ref, ref, sem).wait()

    def edges(block, side):
        own = own_r if side else own_l

        def one_row(r, carry):
            row = block * TILE + r
            mask_i = mask_s[me * rows + row].astype(jnp.float32)
            for kt in range(lane_tiles):
                devs = pl.ds(kt * block_devs, block_devs)
                if side:
                    x = pair[row, devs].reshape(LANES, -1).astype(jnp.float32)
                    nrm = layer_norm(x, 1).astype(jnp.bfloat16)
                    normed[row, devs] = nrm.reshape(block_devs, blocks, TILE, -1)
                else:
                    nrm = normed[row, devs].reshape(LANES, -1)
                h = lax.dot_general(
                    wt[side], nrm, (((1,), (1,)), ((), ())), preferred_element_type=jnp.float32
                )
                mask_k = mask_v[:, kt * LANES : (kt + 1) * LANES].astype(jnp.float32) * mask_i
                stage[kt, pl.ds(r * PITCH, width), :] = sigmoid(h[:width]) * h[width:] * mask_k
            return carry

        lax.fori_loop(0, TILE, one_row, 0)

        def one_channel(c, carry):
            for kt in range(lane_tiles):
                v = stage[kt, pl.ds(c, TILE, stride=PITCH), :]
                own[c, block * TILE : (block + 1) * TILE, kt * LANES : (kt + 1) * LANES] = (
                    v.astype(jnp.bfloat16)
                )
            return carry

        lax.fori_loop(0, width, one_channel, 0, unroll=8)

    def send_edges(block, side, inner):
        sem_own = 0 if inner else 2
        row_block = pl.ds(block * TILE, TILE)
        l_rows = pl.ds(spot * rows + block * TILE, TILE)
        r_rows = pl.ds(spot * TILE, TILE)

        def targets(cls):
            for step in range(plane):
                at = lax.rem(lane + step, plane)
                local = cls == inner and step == 0
                yield at, local, pl.ds(first_channel(cls, at), shares[cls])

        def cross(classes):
            for group in range(GROUPS):
                for cls in classes:
                    part = shares[cls] // GROUPS
                    for at, _, _ in targets(cls):
                        remote(
                            own_r.at[pl.ds(first_channel(cls, at) + group * part, part), row_block],
                            got_r.at[block, 1, pl.ds(group * part, part), r_rows],
                            out_r.at[block], sem_c.at[block, group], device(1 - half, cls, at),
                        )

        def own_right(cls):
            dst = got_r.at[block, 0, pl.ds(0, shares[cls]), r_rows]
            for at, local, channels in targets(cls):
                src = own_r.at[channels, row_block]
                if local:
                    pltpu.make_async_copy(src, dst, sem_r.at[block, sem_own]).start()
                else:
                    remote(
                        src, dst, out_r.at[block], sem_r.at[block, sem_own], device(half, cls, at)
                    )

        def own_left(cls):
            dst = got_l.at[pl.ds(0, shares[cls]), l_rows]
            for at, local, channels in targets(cls):
                src = own_l.at[channels, row_block]
                if local:
                    pltpu.make_async_copy(src, dst, sem_l).start()
                else:
                    remote(src, dst, out_l, sem_l, device(half, cls, at))

        if not side:
            own_left(0)
            own_left(1)
        elif inner:
            cross((1, 0))
            own_right(0)
            own_right(1)
        else:
            own_right(1)
            cross((0,))
            own_right(0)

    def forward(block, inner):
        if inner:
            from_ends = pl.ds(half * plane * TILE, plane * TILE)
            wait(got_r.at[block, 0, pl.ds(0, shares[1]), from_ends], sem_r.at[block, 2])
            part = shares[1] // GROUPS
            for group in range(GROUPS):
                channels = pl.ds(group * part, part)
                remote(
                    got_r.at[block, 0, channels, from_ends],
                    got_r.at[block, 1, channels, from_ends],
                    out_x.at[block], sem_c.at[block, group], device(1 - half, 1, lane),
                )

    def contract(block, rel, inner):
        share = shares[inner]
        groups = GROUPS if rel else 1
        size = share // groups
        if not rel:
            part = got_r.at[block, 0, pl.ds(0, share), pl.ds(0, plane * TILE)]
            wait(part, sem_r.at[block, 0])
            if not inner:
                wait(part, sem_r.at[block, 2])

        def one(c, carry):
            tri[block, rel, c] = lax.dot_general(
                got_l[c], got_r[block, rel, c], (((1,), (1,)), ((), ())),
                preferred_element_type=jnp.float32,
            ).astype(jnp.bfloat16)
            return carry

        for group in range(groups):
            channels = pl.ds(group * size, size)
            if rel:
                wait(got_r.at[block, 1, channels], sem_c.at[block, group])
            lax.fori_loop(group * size, (group + 1) * size, one, 0)
            dst = got_t.at[block, rel, pl.ds(first_channel(inner, lane) + group * size, size)]
            for step in range(1, peers):
                to = lax.rem(spot + step, peers)
                remote(
                    tri.at[block, rel, channels, pl.ds(to * rows, rows)], dst,
                    out_t.at[block, rel], sem_t.at[block, rel], half * peers + to,
                )
            pltpu.make_async_copy(
                tri.at[block, rel, channels, pl.ds(spot * rows, rows)], dst, sem_t.at[block, rel]
            ).start()

    def finish(block, rel):
        pltpu.make_async_copy(
            got_t.at[block, rel], got_t.at[block, rel], sem_t.at[block, rel]
        ).wait()
        source = lax.rem(half + rel, HALVES)
        devs = pl.ds(source * peers, peers)
        for ib in range(rows // TILE):
            i_rows = pl.ds(ib * TILE, TILE)

            def load(c):
                return got_t[block, rel, c, i_rows, :].astype(jnp.float32)

            zero = jnp.zeros((TILE, peers * TILE), jnp.float32)
            mean = lax.fori_loop(0, width, lambda c, s: s + load(c), zero, unroll=8) * (1.0 / width)

            def spread(c, s):
                d = load(c) - mean
                return s + d * d

            var = lax.fori_loop(0, width, spread, zero, unroll=8) * (1.0 / width)
            scale = lax.rsqrt(var + EPS)

            def put(c, carry):
                turn[pl.ds(c * FPITCH, TILE), :] = (load(c) - mean) * scale
                return carry

            lax.fori_loop(0, width, put, 0, unroll=8)

            def one_row(i, carry):
                row = ib * TILE + i
                tn = turn[pl.ds(i, width, stride=FPITCH), :].astype(jnp.bfloat16)
                projected = lax.dot_general(
                    tn, w_out[...], (((0,), (0,)), ((), ())), preferred_element_type=jnp.float32
                )
                nrm = normed[row, devs, block].reshape(peers * TILE, -1)
                gates = sigmoid(jnp.dot(nrm, w_gate[...], preferred_element_type=jnp.float32))
                out[row, devs, block] = (
                    (gates * projected).astype(jnp.bfloat16).reshape(peers, TILE, -1)
                )
                return carry

            lax.fori_loop(0, TILE, one_row, 0, unroll=2)
        pltpu.make_async_copy(
            out.at[:, devs, block], result.at[:, devs, block], sem_out.at[block, rel]
        ).start()

    for side in (1, 0):
        for block in range(blocks):
            edges(block, side)
            if side and block == 0:
                pl.semaphore_wait(barrier, n - 1)
            by_role(functools.partial(send_edges, block, side))

    def ready(inner):
        for block in range(blocks):
            forward(block, inner)
        wait(got_l.at[pl.ds(0, shares[inner])], sem_l)

    by_role(ready)
    steps = [(block, rel) for rel in range(HALVES) for block in range(blocks)]
    for at, step in enumerate(steps):
        by_role(functools.partial(contract, *step))
        if at >= 1:
            finish(*steps[at - 1])
    finish(*steps[-1])

    def drain(inner):
        near = width - shares[inner]
        far = width if inner else plane * shares[0]
        wait(own_l.at[pl.ds(0, near)], out_l)
        for block in range(blocks):
            wait(own_r.at[pl.ds(0, (near + far) // 2)], out_r.at[block])
            if inner:
                wait(got_r.at[block, 0, pl.ds(0, shares[1]), pl.ds(0, plane * TILE)], out_x.at[block])
            for rel in range(HALVES):
                wait(
                    tri.at[block, rel, pl.ds(0, shares[inner]), pl.ds(0, (peers - 1) * rows)],
                    out_t.at[block, rel],
                )

    by_role(drain)
    for block in range(blocks):
        for rel in range(HALVES):
            done = out.at[:, pl.ds(0, peers), block]
            wait(done, sem_out.at[block, rel])


def fused_body(n, pair_act, res_mask, w_left, w_right, w_gate, w_out):
    rows, length, depth = pair_act.shape
    width = w_left.shape[1] // 2
    peers = n // HALVES
    share = max(shares_of(width, peers))
    blocks = rows // TILE
    bf16 = jnp.bfloat16
    view = (rows, n, blocks, TILE, depth)
    vmem = pl.BlockSpec(memory_space=pltpu.VMEM)
    dma = pltpu.SemaphoreType.DMA
    result = pl.pallas_call(
        functools.partial(kernel, n),
        out_shape=jax.ShapeDtypeStruct(view, bf16),
        in_specs=[vmem, pl.BlockSpec(memory_space=pltpu.SMEM)] + [vmem] * 5,
        out_specs=pl.BlockSpec(memory_space=pl.ANY),
        scratch_shapes=[
            pltpu.VMEM(view, bf16),
            pltpu.VMEM((width, rows, length), bf16),
            pltpu.VMEM((width, rows, length), bf16),
            pltpu.VMEM((share, peers * rows, length), bf16),
            pltpu.VMEM((blocks, HALVES, share, peers * TILE, length), bf16),
            pltpu.VMEM((blocks, HALVES, share, peers * rows, peers * TILE), bf16),
            pltpu.VMEM((blocks, HALVES, width, rows, peers * TILE), bf16),
            pltpu.VMEM((length // LANES, TILE * PITCH, LANES), jnp.float32),
            pltpu.VMEM((width * FPITCH, LANES), jnp.float32),
            pltpu.VMEM((2, 2 * width, depth), bf16),
            pltpu.VMEM(view, bf16),
            dma,
            dma((blocks, 3)),
            dma((blocks, GROUPS)),
            dma((blocks, HALVES)),
            dma,
            dma((blocks,)),
            dma((blocks,)),
            dma((blocks, HALVES)),
            dma((blocks, HALVES)),
        ],
        compiler_params=pltpu.CompilerParams(
            collective_id=0, has_side_effects=True, vmem_limit_bytes=62 * 2**20
        ),
    )(pair_act.reshape(view), res_mask, res_mask.reshape(1, length), w_left, w_right, w_gate, w_out)
    return result.reshape(rows, length, depth)


def body(n, pair_act, *others):
    rows, length, depth = pair_act.shape
    fits = rows == 2 * TILE and n // HALVES * TILE == LANES and depth == LANES and length == n * rows
    if fits and others[1].shape[1] == 2 * LANES:
        return fused_body(n, pair_act, *others)
    return plain_body(pair_act, *others)


def solution(mesh):
    placed = (P(("group", "row"), None, None), P("group"), P(), P(), P(), P())
    return jax.shard_map(
        functools.partial(body, mesh.shape["row"]), mesh=mesh, in_specs=placed,
        out_specs=P(("group", "row"), None, None), check_vma=False,
    )
```
